128 devices in a mesh: row: 16 (over z, x_hi, core), col: 8 (over y, x_lo).
Axes of the slice: x: 4 (x_hi: 2, x_lo: 2; x = x_hi * 2 + x_lo), y: 4, z: 4, core: 2. Of those that a mesh axis runs over, the one named last changes fastest.
Arguments:
- image_embed: bfloat16 [65536, 1152], P(('row', 'col')), may hold values from -0.1875 to 0.1875
- text_embed: bfloat16 [65536, 1152], P(('row', 'col')), may hold values from -0.1875 to 0.1875
- partner: int32 [65536], P(('row', 'col')), may hold values from 0 to 65535, each once
- offset: int32 [1], replicated, may hold values from 0 to 127
- log_scale: float32 [1], replicated, may hold values from 2 to 3
- logit_bias: float32 [1], replicated, may hold values from -3 to -1
Outputs:
- row_loss: float32 [65536], P(('row', 'col'))
- image_grad: bfloat16 [65536, 1152], P(('row', 'col'))
- text_grad: bfloat16 [65536, 1152], P(('row', 'col'))
The draws below stay inside these ranges and needn't reach their ends.
Inputs may be any that keep to these rules, and one draw needn't show every extreme that they name: A permutation: every text row is the partner of exactly one image row.
All inputs are finite; a program needn't handle non-finite values.
Results may differ from the reference program's by a relative error of at most 0.0045.
Values may be sent and summed in bfloat16 or wider, within the bound.
A program may use at most 128 MiB of HBM per device.

```python
import jax
import jax.numpy as jnp

D = 1152
TOK_DEV = 512
STEPS = 8
TOKENS = 65536
N_ROW = 16
N_COL = 8


def level_of(rng, shape, shards, smallest, top_value):
    factor_of = 1.0
    for dim, parts in shards:
        heights = jax.random.uniform(jax.random.fold_in(jax.random.fold_in(rng, 6), dim), (parts,), jnp.float32, smallest / len(shards), top_value / len(shards))
        factor_of = factor_of * jnp.repeat(jnp.exp(heights), shape[dim] // parts).reshape((-1,) + (1,) * (len(shape) - 1 - dim))
    return factor_of


def normal_values(stream_key, shape, scale, limit, cuts=(), kind=jnp.bfloat16):
    result = scale * jax.random.normal(stream_key, shape, jnp.float32)
    if cuts:
        result = result * level_of(stream_key, shape, cuts, -0.22, 0.18)
    return jnp.clip(result, -limit, limit).astype(kind)


def setup_inputs(seed: int = 0) -> dict:
    keys = jax.random.split(jax.random.key(seed), 7)
    image_embed = normal_values(keys[0], (TOKENS, D), D ** -0.5, 0.1875, ((0, 128),))
    text_embed = normal_values(keys[1], (TOKENS, D), D ** -0.5, 0.1875, ((0, 128),))
    partner = jax.random.permutation(keys[2], TOKENS).astype(jnp.int32)
    offset = jax.random.randint(keys[3], (1,), 0, N_ROW * N_COL).astype(jnp.int32)
    log_scale = jnp.clip(jax.random.uniform(keys[4], (1,), jnp.float32, 2.0, 3.0), 2.0, 3.0)
    logit_bias = jnp.clip(jax.random.uniform(keys[5], (1,), jnp.float32, -3.0, -1.0), -3.0, -1.0)
    return dict(image_embed=image_embed, text_embed=text_embed, partner=partner, offset=offset, log_scale=log_scale, logit_bias=logit_bias)


def reference(image_embed, text_embed, partner, offset, log_scale, logit_bias):
    blocks = N_ROW * N_COL
    images = image_embed.reshape(blocks, TOK_DEV, D).astype(jnp.float32)
    texts = text_embed.reshape(blocks, TOK_DEV, D)
    partners = partner.reshape(blocks, TOK_DEV)
    logit_scale = jnp.exp(log_scale[0])
    bias_value = logit_bias[0]
    inside = jnp.arange(TOK_DEV, dtype=jnp.int32)
    grad_images = jnp.zeros((blocks, TOK_DEV, D), jnp.float32)
    grad_texts = jnp.zeros((blocks, TOK_DEV, D), jnp.float32)
    loss_total = jnp.zeros((blocks, TOK_DEV), jnp.float32)
    for step_number in range(STEPS):
        source = ((jnp.arange(blocks, dtype=jnp.int32) + offset[0] + step_number) % blocks).astype(jnp.int32)
        held = texts[source].astype(jnp.float32)
        columns = source[:, None] * TOK_DEV + inside[None, :]
        logits = logit_scale * jnp.einsum('pid,pjd->pij', images, held) + bias_value
        labels = jnp.where(partners[:, :, None] == columns[:, None, :], 1.0, -1.0).astype(jnp.float32)
        loss_total = loss_total - jnp.sum(jax.nn.log_sigmoid(labels * logits), axis=2)
        weights = (-labels * jax.nn.sigmoid(-labels * logits) * logit_scale).astype(jnp.bfloat16).astype(jnp.float32)
        grad_images = grad_images + jnp.einsum('pij,pjd->pid', weights, held)
        partial_text = jnp.einsum('pij,pid->pjd', weights, images)
        grad_texts = grad_texts.at[source].add(partial_text)
    row_loss = (loss_total / (STEPS * TOK_DEV)).reshape(blocks * TOK_DEV)
    image_grad = grad_images.reshape(blocks * TOK_DEV, D).astype(jnp.bfloat16)
    text_grad = grad_texts.reshape(blocks * TOK_DEV, D).astype(jnp.bfloat16)
    return (row_loss, image_grad, text_grad)
```

```python
import functools

import jax
import jax.numpy as jnp
from jax import lax
from jax.experimental import pallas as pl
from jax.experimental.pallas import tpu as pltpu
from jax.sharding import PartitionSpec as P

AXES = ("row", "col")
BLOCKS = 128
STEPS = 8
CHUNKS = 4
MESH = pl.DeviceIdType.MESH
F32 = jnp.float32
BF16 = jnp.bfloat16


def place(chip, core):
    z, x_hi = chip // 16, chip // 8 % 2
    step, lane = chip % 8 // 2, chip % 2
    y = step + x_hi * (3 - 2 * step)
    x_lo = lane + x_hi * (1 - 2 * lane)
    return z * 4 + x_hi * 2 + core, y * 2 + x_lo


def home(block):
    row, col = place(block // 2, block % 2)
    return row * 8 + col


def kernel(
    scalars, offset, partner, image, text, loss, image_grad, text_grad,
    texts, image_t, logits, weights, weights_t, grad, own, other,
    from_sib, from_y, from_x, to_y, to_x, loss_sum,
    dist_send, dist_recv, red_send, red_recv,
):
    rows, depth = image.shape
    size = rows // CHUNKS
    row, col = lax.axis_index("row"), lax.axis_index("col")
    z, x_hi, core = row // 4, row // 2 % 2, row % 2
    y, x_lo = col // 2, col % 2
    step = y + x_hi * (3 - 2 * y)
    lane = x_lo + x_hi * (1 - 2 * x_lo)
    chip = z * 16 + x_hi * 8 + 2 * step + lane
    behind = place((chip + 62) % 64, core)
    ahead = place((chip + 2) % 64, core)
    across = place(chip + 1 - 2 * lane, core)
    sibling = (row + 1 - 2 * core, col)

    barrier = pltpu.get_barrier_semaphore()
    for device in (behind, ahead, across, sibling):
        pl.semaphore_signal(barrier, inc=1, device_id=device, device_id_type=MESH)
    pl.semaphore_wait(barrier, 4)

    def slot(s):
        return pl.ds(pl.multiple_of(s * size, size), size)

    def copy(src, dst, send, recv, kind, c, device):
        return pltpu.make_async_remote_copy(
            src_ref=src, dst_ref=dst, send_sem=send.at[c, kind], recv_sem=recv.at[c, kind],
            device_id=device, device_id_type=MESH,
        )

    def d_back(c, s):
        place_of = (0, 1, 2)[s]
        target = (2, 3, 8)[s]
        return copy(texts.at[c, slot(place_of)], texts.at[c, slot(target)], dist_send, dist_recv, s, c, behind)

    def d_across(c):
        return copy(texts.at[c, slot(2 - 2 * lane)], texts.at[c, slot(1)], dist_send, dist_recv, 3, c, across)

    def d_sib(c, k):
        s = k + 1 - core
        return copy(
            texts.at[c, slot(s + 4 * (s // 4))], texts.at[c, slot(4 + k)], dist_send, dist_recv, 4 + k, c, sibling
        )

    def dist_start(c):
        texts[c, slot(0)] = text[slot(c)]
        d_back(c, 0).start()

        @pl.when(lane == 1)
        def _():
            d_across(c).start()

        @pl.when(core == 1)
        def _():
            d_sib(c, 0).start()

    def dist_mid(c):
        d_back(c, 0).wait_recv()

        @pl.when(core == 0)
        def _():
            d_back(c, 2).start()
            d_sib(c, 1).start()

        @pl.when(core == 1)
        def _():
            d_sib(c, 2).start()

        @pl.when(lane == 0)
        def _():
            d_across(c).start()

        d_across(c).wait_recv()
        d_back(c, 1).start()

        @pl.when(core == 0)
        def _():
            d_sib(c, 0).start()

        @pl.when(core == 1)
        def _():
            d_sib(c, 1).start()

    def dist_late(c):
        d_back(c, 1).wait_recv()

        @pl.when(core == 0)
        def _():
            d_sib(c, 2).start()
            d_back(c, 2).wait_recv()
            d_sib(c, 3).start()

        @pl.when(core == 1)
        def _():
            d_sib(c, 3).start()

    def r_ahead(c, t):
        source = from_sib.at[c, slot(3)] if t == 2 else to_y.at[c, slot(t)]
        return copy(source, from_y.at[c, slot(t)], red_send, red_recv, t, c, ahead)

    def r_across(c):
        return copy(to_x.at[c], from_x.at[c], red_send, red_recv, 3, c, across)

    def r_sib(c, k):
        return copy(other.at[c, slot(k)], from_sib.at[c, slot(k)], red_send, red_recv, 4 + k, c, sibling)

    scale, bias = scalars[0], scalars[1]
    tile = 2 * size
    part = 32

    def compute(c):
        for k in range(4):
            d_sib(c, k).wait_recv()

        def logits_step(i, _):
            at = pl.ds(pl.multiple_of(i * tile, tile), tile)
            logits[...] = jnp.dot(texts[c, at], image_t[...], preferred_element_type=F32)

            def part_step(j, carry):
                excess, linear = carry
                here = pl.ds(pl.multiple_of(j * part, part), part)
                sigma = 2 * i + j * part // size
                block = (2 * chip + core + 2 * (sigma % 4) + sigma // 4 + offset[0]) % BLOCKS
                first = block * rows + c * size + j * part % size
                match = partner[...] - first == lax.broadcasted_iota(jnp.int32, (part, rows), 0)
                x = logits[here] * scale + bias
                u = jnp.exp(-jnp.abs(x))
                r = 1.0 / (1.0 + u)
                sig = jnp.where(x >= 0.0, r, u * r)
                w = jnp.where(match, sig - 1.0, sig) * scale
                weights[pl.ds(pl.multiple_of(i * tile + j * part, part), part)] = w.astype(BF16)
                lin = jnp.maximum(x, 0.0) - jnp.where(match, x, 0.0)
                for g in range(part // 8):
                    ug = u[8 * g : 8 * g + 8]
                    excess = excess + ug * (1.0 + excess)
                    linear = linear + lin[8 * g : 8 * g + 8]
                return excess, linear

            zero = jnp.zeros((8, rows), F32)
            excess, linear = lax.fori_loop(0, tile // part, part_step, (zero, zero))
            loss_sum[...] += linear + jnp.log1p(excess)
            weights_t[:, at] = weights[at].T
            return 0

        lax.fori_loop(0, 4, logits_step, 0)

        for k in range(4):
            at = pl.ds((4 + k) * size, size)
            other[c, slot(k)] = jnp.dot(weights[at], image[...], preferred_element_type=F32).astype(BF16)
            r_sib(c, k).start()
        for k in range(4):
            at = pl.ds(k * size, size)
            own[c, at] = jnp.dot(weights[at], image[...], preferred_element_type=F32)
        width = 384
        for d in range(depth // width):
            columns = pl.ds(d * width, width)
            part_grad = jnp.dot(weights_t[...], texts[c, pl.ds(0, 8 * size), columns], preferred_element_type=F32)
            if c == 0:
                grad[:, columns] = part_grad
            else:
                grad[:, columns] += part_grad

    def red_1(c):
        for k in range(4):
            r_sib(c, k).wait_recv()

        @pl.when(core == 0)
        def _():
            r_ahead(c, 2).start()

        to_y[c, slot(1)] = (own[c, slot(3)] + from_sib[c, slot(2 + core)].astype(F32)).astype(BF16)
        r_ahead(c, 1).start()

    def red_2(c):
        r_ahead(c, 1).wait_recv()
        to_x[c] = (
            own[c, slot(1)] + from_sib[c, slot(core)].astype(F32) + from_y[c, slot(1)].astype(F32)
        ).astype(BF16)
        r_across(c).start()
        own[c, slot(2)] += from_sib[c, slot(1 + core)].astype(F32)

        @pl.when(core == 0)
        def _():
            r_ahead(c, 2).wait_recv()
            own[c, slot(2)] += from_y[c, slot(2)].astype(F32)

        @pl.when(lane == 1)
        def _():
            to_y[c, slot(0)] = own[c, slot(2)].astype(BF16)
            r_ahead(c, 0).start()

    def red_3(c):
        r_across(c).wait_recv()

        @pl.when(lane == 0)
        def _():
            to_y[c, slot(0)] = (own[c, slot(2)] + from_x[c].astype(F32)).astype(BF16)
            r_ahead(c, 0).start()

        @pl.when(lane == 1)
        def _():
            own[c, slot(0)] += from_x[c].astype(F32)

        @pl.when(core == 1)
        def _():
            own[c, slot(0)] += from_sib[c, slot(0)].astype(F32)

    def red_4(c):
        r_ahead(c, 0).wait_recv()
        text_grad[slot(c)] = (own[c, slot(0)] + from_y[c, slot(0)].astype(F32)).astype(BF16)

    dist_start(0)
    loss_sum[...] = jnp.zeros_like(loss_sum)
    image_t[...] = image[...].T
    dist_mid(0)
    dist_start(1)
    dist_late(0)
    for c in range(CHUNKS):
        if c + 1 < CHUNKS:
            dist_mid(c + 1)
        if c + 2 < CHUNKS:
            dist_start(c + 2)
        compute(c)
        red_1(c)
        if c >= 1:
            red_2(c - 1)
            red_3(c - 1)
        if c >= 2:
            red_4(c - 2)
        if c + 1 < CHUNKS:
            dist_late(c + 1)
    image_grad[...] = grad[...].astype(BF16)
    loss[...] = jnp.sum(loss_sum[...], axis=0, keepdims=True) * (1.0 / (STEPS * rows))
    red_4(CHUNKS - 2)
    red_2(CHUNKS - 1)
    red_3(CHUNKS - 1)
    red_4(CHUNKS - 1)

    for c in range(CHUNKS):
        d_back(c, 0).wait_send()
        d_back(c, 1).wait_send()
        d_across(c).wait_send()
        r_ahead(c, 0).wait_send()
        r_ahead(c, 1).wait_send()
        r_across(c).wait_send()

        @pl.when(core == 0)
        def _():
            d_back(c, 2).wait_send()
            r_ahead(c, 2).wait_send()

        for k in range(4):
            d_sib(c, k).wait_send()
            r_sib(c, k).wait_send()


def window_terms(scalars, offset, partner, image, text):
    rows, depth = image.shape
    size = rows // CHUNKS
    vmem = pl.BlockSpec(memory_space=pltpu.VMEM)
    smem = pl.BlockSpec(memory_space=pltpu.SMEM)
    return pl.pallas_call(
        kernel,
        name="window_terms",
        out_shape=(
            jax.ShapeDtypeStruct((1, rows), F32),
            jax.ShapeDtypeStruct((rows, depth), BF16),
            jax.ShapeDtypeStruct((rows, depth), BF16),
        ),
        in_specs=[smem, smem, vmem, vmem, vmem],
        out_specs=[vmem, vmem, vmem],
        scratch_shapes=[
            pltpu.VMEM((CHUNKS, 9 * size, depth), BF16),
            pltpu.VMEM((depth, rows), BF16),
            pltpu.VMEM((2 * size, rows), F32),
            pltpu.VMEM((8 * size, rows), BF16),
            pltpu.VMEM((rows, 8 * size), BF16),
            pltpu.VMEM((rows, depth), F32),
            pltpu.VMEM((CHUNKS, 4 * size, depth), F32),
            pltpu.VMEM((CHUNKS, 4 * size, depth), BF16),
            pltpu.VMEM((CHUNKS, 4 * size, depth), BF16),
            pltpu.VMEM((CHUNKS, 3 * size, depth), BF16),
            pltpu.VMEM((CHUNKS, size, depth), BF16),
            pltpu.VMEM((CHUNKS, 2 * size, depth), BF16),
            pltpu.VMEM((CHUNKS, size, depth), BF16),
            pltpu.VMEM((8, rows), F32),
            pltpu.SemaphoreType.DMA((CHUNKS, 8)),
            pltpu.SemaphoreType.DMA((CHUNKS, 8)),
            pltpu.SemaphoreType.DMA((CHUNKS, 8)),
            pltpu.SemaphoreType.DMA((CHUNKS, 8)),
        ],
        compiler_params=pltpu.CompilerParams(
            collective_id=0, has_side_effects=True, vmem_limit_bytes=60 * 2**20
        ),
        cost_estimate=pl.CostEstimate(
            flops=3 * 2 * STEPS * rows * rows * depth,
            bytes_accessed=8 * rows * depth,
            transcendentals=2 * STEPS * rows * rows,
        ),
    )(scalars, offset, partner, image, text)


def moved_by(offset, values, pairs_for):
    branches = [
        functools.partial(lambda pairs, v: lax.ppermute(v, AXES, pairs), pairs_for(by)) for by in range(BLOCKS)
    ]
    return lax.switch(offset, branches, values)


def on_device(image_embed, text_embed, partner, offset, log_scale, logit_bias):
    rows = image_embed.shape[0]
    start = offset % BLOCKS
    out = [(block, home(block)) for block in range(BLOCKS)]
    back = [(there, here) for here, there in out]
    image = lax.ppermute(image_embed, AXES, out)
    partner = lax.ppermute(partner, AXES, out)
    text = moved_by(start[0], text_embed, lambda by: [(t, home((t - by) % BLOCKS)) for t in range(BLOCKS)])
    scalars = jnp.concatenate([jnp.exp(log_scale), logit_bias])
    loss, image_grad, text_grad = window_terms(scalars, start, partner.reshape(1, rows), image, text)
    row_loss = lax.ppermute(loss.reshape(rows), AXES, back)
    image_grad = lax.ppermute(image_grad, AXES, back)
    text_grad = moved_by(
        start[0], text_grad, lambda by: [(home((t - by) % BLOCKS), t) for t in range(BLOCKS)]
    )
    return row_loss, image_grad, text_grad


def solution(mesh):
    return jax.shard_map(
        on_device,
        mesh=mesh,
        in_specs=(P(AXES, None), P(AXES, None), P(AXES), P(), P(), P()),
        out_specs=(P(AXES), P(AXES, None), P(AXES, None)),
        check_vma=False,
    )
```

```python
import functools

import jax
import jax.numpy as jnp
from jax import lax
from jax.experimental import pallas as pl
from jax.experimental.pallas import tpu as pltpu
from jax.sharding import PartitionSpec as P

AXES = ("row", "col")
BLOCKS = 128
STEPS = 8
CHUNKS = 8
STAGES = (0.0, 1.5, 2.2, 3.0, 3.6, 4.0, 5.0, 6.0, 7.0)
MESH = pl.DeviceIdType.MESH
F32 = jnp.float32
BF16 = jnp.bfloat16


def place(chip, core):
    z, x_hi = chip // 16, chip // 8 % 2
    step, lane = chip % 8 // 2, chip % 2
    y = step + x_hi * (3 - 2 * step)
    x_lo = lane + x_hi * (1 - 2 * lane)
    return z * 4 + x_hi * 2 + core, y * 2 + x_lo


def home(block):
    row, col = place(block // 2, block % 2)
    return row * 8 + col


def kernel(
    scalars, offset, partner, image, text, loss, image_grad, text_grad,
    texts, image_t, logits, weights, weights_t, grad, own, other,
    from_sib, from_y, from_x, to_y, to_x, loss_sum,
    dist_send, dist_recv, red_send, red_recv,
):
    rows, depth = image.shape
    size = rows // CHUNKS
    row, col = lax.axis_index("row"), lax.axis_index("col")
    z, x_hi, core = row // 4, row // 2 % 2, row % 2
    y, x_lo = col // 2, col % 2
    step = y + x_hi * (3 - 2 * y)
    lane = x_lo + x_hi * (1 - 2 * x_lo)
    chip = z * 16 + x_hi * 8 + 2 * step + lane
    behind = place((chip + 62) % 64, core)
    ahead = place((chip + 2) % 64, core)
    across = place(chip + 1 - 2 * lane, core)
    sibling = (row + 1 - 2 * core, col)

    barrier = pltpu.get_barrier_semaphore()
    for device in (behind, ahead, across, sibling):
        pl.semaphore_signal(barrier, inc=1, device_id=device, device_id_type=MESH)
    pl.semaphore_wait(barrier, 4)

    def slot(s):
        return pl.ds(pl.multiple_of(s * size, size), size)

    def copy(src, dst, send, recv, kind, c, device):
        return pltpu.make_async_remote_copy(
            src_ref=src, dst_ref=dst, send_sem=send.at[c, kind], recv_sem=recv.at[c, kind],
            device_id=device, device_id_type=MESH,
        )

    def d_back(c, s):
        place_of = (0, 1, 2)[s]
        target = (2, 3, 8)[s]
        return copy(texts.at[c, slot(place_of)], texts.at[c, slot(target)], dist_send, dist_recv, s, c, behind)

    def d_across(c):
        return copy(texts.at[c, slot(2 - 2 * lane)], texts.at[c, slot(1)], dist_send, dist_recv, 3, c, across)

    def d_sib(c, k):
        s = k + 1 - core
        return copy(
            texts.at[c, slot(s + 4 * (s // 4))], texts.at[c, slot(4 + k)], dist_send, dist_recv, 4 + k, c, sibling
        )

    def dist_start(c):
        texts[c, slot(0)] = text[slot(c)]
        d_back(c, 0).start()

        @pl.when(lane == 1)
        def _():
            d_across(c).start()

        @pl.when(core == 1)
        def _():
            d_sib(c, 0).start()

    def dist_second(c):
        d_back(c, 0).wait_recv()

        @pl.when(core == 0)
        def _():
            d_back(c, 2).start()
            d_sib(c, 1).start()

        @pl.when(core == 1)
        def _():
            d_sib(c, 2).start()

        @pl.when(lane == 0)
        def _():
            d_across(c).start()

    def dist_third(c):
        d_across(c).wait_recv()
        d_back(c, 1).start()

        @pl.when(core == 0)
        def _():
            d_sib(c, 0).start()

        @pl.when(core == 1)
        def _():
            d_sib(c, 1).start()

    def dist_late(c):
        d_back(c, 1).wait_recv()

        @pl.when(core == 0)
        def _():
            d_sib(c, 2).start()
            d_back(c, 2).wait_recv()
            d_sib(c, 3).start()

        @pl.when(core == 1)
        def _():
            d_sib(c, 3).start()

    def r_ahead(c, t):
        source = from_sib.at[c, slot(3)] if t == 2 else to_y.at[c, slot(t)]
        return copy(source, from_y.at[c, slot(t)], red_send, red_recv, t, c, ahead)

    def r_across(c):
        return copy(to_x.at[c], from_x.at[c], red_send, red_recv, 3, c, across)

    def r_sib(c, k):
        return copy(other.at[c, slot(k)], from_sib.at[c, slot(k)], red_send, red_recv, 4 + k, c, sibling)

    scale, bias = scalars[0], scalars[1]
    tile = 2 * size
    part = 32

    def compute(c):
        for k in range(4):
            d_sib(c, k).wait_recv()

        def logits_step(i, _):
            at = pl.ds(pl.multiple_of(i * tile, tile), tile)
            logits[...] = jnp.dot(texts[c, at], image_t[...], preferred_element_type=F32)

            def part_step(j, carry):
                excess, linear = carry
                here = pl.ds(pl.multiple_of(j * part, part), part)
                sigma = 2 * i + j * part // size
                block = (2 * chip + core + 2 * (sigma % 4) + sigma // 4 + offset[0]) % BLOCKS
                first = block * rows + c * size + j * part % size
                match = partner[...] - first == lax.broadcasted_iota(jnp.int32, (part, rows), 0)
                x = logits[here] * scale + bias
                u = jnp.exp(-jnp.abs(x))
                r = 1.0 / (1.0 + u)
                sig = jnp.where(x >= 0.0, r, u * r)
                w = jnp.where(match, sig - 1.0, sig) * scale
                weights[pl.ds(pl.multiple_of(i * tile + j * part, part), part)] = w.astype(BF16)
                lin = jnp.maximum(x, 0.0) - jnp.where(match, x, 0.0)
                for g in range(part // 8):
                    ug = u[8 * g : 8 * g + 8]
                    excess = excess + ug * (1.0 + excess)
                    linear = linear + lin[8 * g : 8 * g + 8]
                return excess, linear

            zero = jnp.zeros((8, rows), F32)
            excess, linear = lax.fori_loop(0, tile // part, part_step, (zero, zero))
            loss_sum[...] += linear + jnp.log1p(excess)
            weights_t[:, at] = weights[at].T
            return 0

        lax.fori_loop(0, 4, logits_step, 0)

        for k in range(4):
            at = pl.ds((4 + k) * size, size)
            other[c, slot(k)] = jnp.dot(weights[at], image[...], preferred_element_type=F32).astype(BF16)
            r_sib(c, k).start()
        for k in range(4):
            at = pl.ds(k * size, size)
            own[c, at] = jnp.dot(weights[at], image[...], preferred_element_type=F32)
        width = 384
        for d in range(depth // width):
            columns = pl.ds(d * width, width)
            part_grad = jnp.dot(weights_t[...], texts[c, pl.ds(0, 8 * size), columns], preferred_element_type=F32)
            if c == 0:
                grad[:, columns] = part_grad
            else:
                grad[:, columns] += part_grad

    def red_1(c):
        for k in range(4):
            r_sib(c, k).wait_recv()

        @pl.when(core == 0)
        def _():
            r_ahead(c, 2).start()

        to_y[c, slot(1)] = (own[c, slot(3)] + from_sib[c, slot(2 + core)].astype(F32)).astype(BF16)
        r_ahead(c, 1).start()

    def red_2(c):
        r_ahead(c, 1).wait_recv()
        to_x[c] = (
            own[c, slot(1)] + from_sib[c, slot(core)].astype(F32) + from_y[c, slot(1)].astype(F32)
        ).astype(BF16)
        r_across(c).start()
        own[c, slot(2)] += from_sib[c, slot(1 + core)].astype(F32)

        @pl.when(core == 0)
        def _():
            r_ahead(c, 2).wait_recv()
            own[c, slot(2)] += from_y[c, slot(2)].astype(F32)

        @pl.when(lane == 1)
        def _():
            to_y[c, slot(0)] = own[c, slot(2)].astype(BF16)
            r_ahead(c, 0).start()

    def red_3(c):
        r_across(c).wait_recv()

        @pl.when(lane == 0)
        def _():
            to_y[c, slot(0)] = (own[c, slot(2)] + from_x[c].astype(F32)).astype(BF16)
            r_ahead(c, 0).start()

        @pl.when(lane == 1)
        def _():
            own[c, slot(0)] += from_x[c].astype(F32)

        @pl.when(core == 1)
        def _():
            own[c, slot(0)] += from_sib[c, slot(0)].astype(F32)

    def red_4(c):
        r_ahead(c, 0).wait_recv()
        text_grad[slot(c)] = (own[c, slot(0)] + from_y[c, slot(0)].astype(F32)).astype(BF16)

    loss_sum[...] = jnp.zeros_like(loss_sum)
    stages = (dist_start, dist_second, dist_third, dist_late, compute, red_1, red_2, red_3, red_4)
    order = sorted((c + when, i, c) for i, when in enumerate(STAGES) for c in range(CHUNKS))
    for _, i, c in order:
        stages[i](c)
        if (i, c) == (0, 0):
            image_t[...] = image[...].T
        if (i, c) == (4, CHUNKS - 1):
            image_grad[...] = grad[...].astype(BF16)
            loss[...] = jnp.sum(loss_sum[...], axis=0, keepdims=True) * (1.0 / (STEPS * rows))

    for c in range(CHUNKS):
        d_back(c, 0).wait_send()
        d_back(c, 1).wait_send()
        d_across(c).wait_send()
        r_ahead(c, 0).wait_send()
        r_ahead(c, 1).wait_send()
        r_across(c).wait_send()

        @pl.when(core == 0)
        def _():
            d_back(c, 2).wait_send()
            r_ahead(c, 2).wait_send()

        for k in range(4):
            d_sib(c, k).wait_send()
            r_sib(c, k).wait_send()


def window_terms(scalars, offset, partner, image, text):
    rows, depth = image.shape
    size = rows // CHUNKS
    vmem = pl.BlockSpec(memory_space=pltpu.VMEM)
    smem = pl.BlockSpec(memory_space=pltpu.SMEM)
    return pl.pallas_call(
        kernel,
        name="window_terms",
        out_shape=(
            jax.ShapeDtypeStruct((1, rows), F32),
            jax.ShapeDtypeStruct((rows, depth), BF16),
            jax.ShapeDtypeStruct((rows, depth), BF16),
        ),
        in_specs=[smem, smem, vmem, vmem, vmem],
        out_specs=[vmem, vmem, vmem],
        scratch_shapes=[
            pltpu.VMEM((CHUNKS, 9 * size, depth), BF16),
            pltpu.VMEM((depth, rows), BF16),
            pltpu.VMEM((2 * size, rows), F32),
            pltpu.VMEM((8 * size, rows), BF16),
            pltpu.VMEM((rows, 8 * size), BF16),
            pltpu.VMEM((rows, depth), F32),
            pltpu.VMEM((CHUNKS, 4 * size, depth), F32),
            pltpu.VMEM((CHUNKS, 4 * size, depth), BF16),
            pltpu.VMEM((CHUNKS, 4 * size, depth), BF16),
            pltpu.VMEM((CHUNKS, 3 * size, depth), BF16),
            pltpu.VMEM((CHUNKS, size, depth), BF16),
            pltpu.VMEM((CHUNKS, 2 * size, depth), BF16),
            pltpu.VMEM((CHUNKS, size, depth), BF16),
            pltpu.VMEM((8, rows), F32),
            pltpu.SemaphoreType.DMA((CHUNKS, 8)),
            pltpu.SemaphoreType.DMA((CHUNKS, 8)),
            pltpu.SemaphoreType.DMA((CHUNKS, 8)),
            pltpu.SemaphoreType.DMA((CHUNKS, 8)),
        ],
        compiler_params=pltpu.CompilerParams(
            collective_id=0, has_side_effects=True, vmem_limit_bytes=60 * 2**20
        ),
        cost_estimate=pl.CostEstimate(
            flops=3 * 2 * STEPS * rows * rows * depth,
            bytes_accessed=8 * rows * depth,
            transcendentals=2 * STEPS * rows * rows,
        ),
    )(scalars, offset, partner, image, text)


def halves(x, n):
    return lax.div(x, n), lax.rem(x, n)


def home_of(block):
    chip, core = halves(block, 2)
    group, inside = halves(chip, 8)
    z, x_hi = halves(group, 2)
    step, lane = halves(inside, 2)
    y = step + x_hi * (3 - 2 * step)
    x_lo = lane + x_hi * (1 - 2 * lane)
    return z * 32 + x_hi * 16 + core * 8 + y * 2 + x_lo


def block_at(row, col):
    z, rest = halves(row, 4)
    x_hi, core = halves(rest, 2)
    y, x_lo = halves(col, 2)
    step = y + x_hi * (3 - 2 * y)
    lane = x_lo + x_hi * (1 - 2 * x_lo)
    return z * 32 + x_hi * 16 + 4 * step + 2 * lane + core


def move_kernel(by, returns, source, target, local, send, recv):
    row, col = lax.axis_index("row"), lax.axis_index("col")
    here = row * 8 + col
    realigned = home_of(lax.rem(here + (BLOCKS - by), BLOCKS))
    original = lax.rem(block_at(row, col) + by, BLOCKS)
    to, fro = (original, realigned) if returns else (realigned, original)
    barrier = pltpu.get_barrier_semaphore()
    remote = pltpu.make_async_remote_copy(
        src_ref=source, dst_ref=target, send_sem=send, recv_sem=recv,
        device_id=halves(to, 8), device_id_type=MESH,
    )

    @pl.when(fro != here)
    def _():
        pl.semaphore_signal(barrier, inc=1, device_id=halves(fro, 8), device_id_type=MESH)

    @pl.when(to != here)
    def _():
        pl.semaphore_wait(barrier, 1)
        remote.start()
        remote.wait_send()

    @pl.when(to == here)
    def _():
        stays = pltpu.make_async_copy(source, target, local)
        stays.start()
        stays.wait()

    @pl.when(fro != here)
    def _():
        remote.wait_recv()


def moved_by(by, values, returns):
    anywhere = pl.BlockSpec(memory_space=pl.ANY)

    def branch(amount):
        return lambda v: pl.pallas_call(
            functools.partial(move_kernel, amount, returns),
            name="move",
            out_shape=jax.ShapeDtypeStruct(v.shape, v.dtype),
            in_specs=[anywhere],
            out_specs=anywhere,
            scratch_shapes=[pltpu.SemaphoreType.DMA] * 3,
            compiler_params=pltpu.CompilerParams(
                collective_id=1 + amount + returns * BLOCKS, has_side_effects=True
            ),
        )(v)

    return lax.switch(by, [branch(amount) for amount in range(BLOCKS)], values)


def on_device(image_embed, text_embed, partner, offset, log_scale, logit_bias):
    rows = image_embed.shape[0]
    start = offset % BLOCKS
    out = [(block, home(block)) for block in range(BLOCKS)]
    back = [(there, here) for here, there in out]
    image = lax.ppermute(image_embed, AXES, out)
    partner = lax.ppermute(partner, AXES, out)
    text = moved_by(start[0], text_embed, False)
    scalars = jnp.concatenate([jnp.exp(log_scale), logit_bias])
    loss, image_grad, text_grad = window_terms(scalars, start, partner.reshape(1, rows), image, text)
    row_loss = lax.ppermute(loss.reshape(rows), AXES, back)
    image_grad = lax.ppermute(image_grad, AXES, back)
    text_grad = moved_by(start[0], text_grad, True)
    return row_loss, image_grad, text_grad


def solution(mesh):
    return jax.shard_map(
        on_device,
        mesh=mesh,
        in_specs=(P(AXES, None), P(AXES, None), P(AXES), P(), P(), P()),
        out_specs=(P(AXES), P(AXES, None), P(AXES, None)),
        check_vma=False,
    )
```

```python
import functools

import jax
import jax.numpy as jnp
from jax import lax
from jax.experimental import pallas as pl
from jax.experimental.pallas import tpu as pltpu
from jax.sharding import PartitionSpec as P

AXES = ("row", "col")
BLOCKS = 128
STEPS = 8
CHUNKS = 8
STAGES = (0.0, 1.5, 2.2, 3.0, 3.6, 4.0, 5.0, 6.0, 7.0)
MESH = pl.DeviceIdType.MESH
F32 = jnp.float32
BF16 = jnp.bfloat16


def place(chip, core):
    z, x_hi = chip // 16, chip // 8 % 2
    step, lane = chip % 8 // 2, chip % 2
    y = (step + x_hi * (3 - 2 * step) + 1) % 4
    x_lo = lane + x_hi * (1 - 2 * lane)
    return z * 4 + x_hi * 2 + core, y * 2 + x_lo


def home(block):
    row, col = place(block // 2, block % 2)
    return row * 8 + col


def kernel(
    scalars, offset, partner, image, text, loss, image_grad, text_grad,
    texts, image_t, logits, weights, weights_t, grad, own, other,
    from_sib, from_y, from_x, to_y, to_x, loss_sum,
    dist_send, dist_recv, red_send, red_recv,
):
    rows, depth = image.shape
    size = rows // CHUNKS
    row, col = lax.axis_index("row"), lax.axis_index("col")
    z, x_hi, core = row // 4, row // 2 % 2, row % 2
    y, x_lo = (col // 2 + 3) % 4, col % 2
    step = y + x_hi * (3 - 2 * y)
    lane = x_lo + x_hi * (1 - 2 * x_lo)
    chip = z * 16 + x_hi * 8 + 2 * step + lane
    behind = place((chip + 62) % 64, core)
    ahead = place((chip + 2) % 64, core)
    across = place(chip + 1 - 2 * lane, core)
    sibling = (row + 1 - 2 * core, col)

    barrier = pltpu.get_barrier_semaphore()
    for device in (behind, ahead, across, sibling):
        pl.semaphore_signal(barrier, inc=1, device_id=device, device_id_type=MESH)
    pl.semaphore_wait(barrier, 4)

    def slot(s):
        return pl.ds(pl.multiple_of(s * size, size), size)

    def copy(src, dst, send, recv, kind, c, device):
        return pltpu.make_async_remote_copy(
            src_ref=src, dst_ref=dst, send_sem=send.at[c, kind], recv_sem=recv.at[c, kind],
            device_id=device, device_id_type=MESH,
        )

    def d_back(c, s):
        place_of = (0, 1, 2)[s]
        target = (2, 3, 8)[s]
        return copy(texts.at[c, slot(place_of)], texts.at[c, slot(target)], dist_send, dist_recv, s, c, behind)

    def d_across(c):
        return copy(texts.at[c, slot(2 - 2 * lane)], texts.at[c, slot(1)], dist_send, dist_recv, 3, c, across)

    def d_sib(c, k):
        s = k + 1 - core
        return copy(
            texts.at[c, slot(s + 4 * (s // 4))], texts.at[c, slot(4 + k)], dist_send, dist_recv, 4 + k, c, sibling
        )

    def dist_start(c):
        texts[c, slot(0)] = text[slot(c)]
        d_back(c, 0).start()

        @pl.when(lane == 1)
        def _():
            d_across(c).start()

        @pl.when(core == 1)
        def _():
            d_sib(c, 0).start()

    def dist_second(c):
        d_back(c, 0).wait_recv()

        @pl.when(core == 0)
        def _():
            d_back(c, 2).start()
            d_sib(c, 1).start()

        @pl.when(core == 1)
        def _():
            d_sib(c, 2).start()

        @pl.when(lane == 0)
        def _():
            d_across(c).start()

    def dist_third(c):
        d_across(c).wait_recv()
        d_back(c, 1).start()

        @pl.when(core == 0)
        def _():
            d_sib(c, 0).start()

        @pl.when(core == 1)
        def _():
            d_sib(c, 1).start()

    def dist_late(c):
        d_back(c, 1).wait_recv()

        @pl.when(core == 0)
        def _():
            d_sib(c, 2).start()
            d_back(c, 2).wait_recv()
            d_sib(c, 3).start()

        @pl.when(core == 1)
        def _():
            d_sib(c, 3).start()

    def r_ahead(c, t):
        source = from_sib.at[c, slot(3)] if t == 2 else to_y.at[c, slot(t)]
        return copy(source, from_y.at[c, slot(t)], red_send, red_recv, t, c, ahead)

    def r_across(c):
        return copy(to_x.at[c], from_x.at[c], red_send, red_recv, 3, c, across)

    def r_sib(c, k):
        return copy(other.at[c, slot(k)], from_sib.at[c, slot(k)], red_send, red_recv, 4 + k, c, sibling)

    scale, bias = scalars[0], scalars[1]
    tile = 2 * size
    part = 32

    def compute(c):
        for k in range(4):
            d_sib(c, k).wait_recv()

        def logits_step(i, _):
            at = pl.ds(pl.multiple_of(i * tile, tile), tile)
            logits[...] = jnp.dot(texts[c, at], image_t[...], preferred_element_type=F32)

            def part_step(j, carry):
                excess, linear = carry
                here = pl.ds(pl.multiple_of(j * part, part), part)
                sigma = 2 * i + j * part // size
                block = (2 * chip + core + 2 * (sigma % 4) + sigma // 4 + offset[0]) % BLOCKS
                first = block * rows + c * size + j * part % size
                match = partner[...] - first == lax.broadcasted_iota(jnp.int32, (part, rows), 0)
                x = logits[here] * scale + bias
                u = jnp.exp(-jnp.abs(x))
                r = 1.0 / (1.0 + u)
                sig = jnp.where(x >= 0.0, r, u * r)
                w = jnp.where(match, sig - 1.0, sig) * scale
                weights[pl.ds(pl.multiple_of(i * tile + j * part, part), part)] = w.astype(BF16)
                lin = jnp.maximum(x, 0.0) - jnp.where(match, x, 0.0)
                for g in range(part // 8):
                    ug = u[8 * g : 8 * g + 8]
                    excess = excess + ug * (1.0 + excess)
                    linear = linear + lin[8 * g : 8 * g + 8]
                return excess, linear

            zero = jnp.zeros((8, rows), F32)
            excess, linear = lax.fori_loop(0, tile // part, part_step, (zero, zero))
            loss_sum[...] += linear + jnp.log1p(excess)
            weights_t[:, at] = weights[at].T
            return 0

        lax.fori_loop(0, 4, logits_step, 0)

        for k in range(4):
            at = pl.ds((4 + k) * size, size)
            other[c, slot(k)] = jnp.dot(weights[at], image[...], preferred_element_type=F32).astype(BF16)
            r_sib(c, k).start()
        for k in range(4):
            at = pl.ds(k * size, size)
            own[c, at] = jnp.dot(weights[at], image[...], preferred_element_type=F32)
        width = 384
        for d in range(depth // width):
            columns = pl.ds(d * width, width)
            part_grad = jnp.dot(weights_t[...], texts[c, pl.ds(0, 8 * size), columns], preferred_element_type=F32)
            if c == 0:
                grad[:, columns] = part_grad
            else:
                grad[:, columns] += part_grad

    def red_1(c):
        for k in range(4):
            r_sib(c, k).wait_recv()

        @pl.when(core == 0)
        def _():
            r_ahead(c, 2).start()

        to_y[c, slot(1)] = (own[c, slot(3)] + from_sib[c, slot(2 + core)].astype(F32)).astype(BF16)
        r_ahead(c, 1).start()

    def red_2(c):
        r_ahead(c, 1).wait_recv()
        to_x[c] = (
            own[c, slot(1)] + from_sib[c, slot(core)].astype(F32) + from_y[c, slot(1)].astype(F32)
        ).astype(BF16)
        r_across(c).start()
        own[c, slot(2)] += from_sib[c, slot(1 + core)].astype(F32)

        @pl.when(core == 0)
        def _():
            r_ahead(c, 2).wait_recv()
            own[c, slot(2)] += from_y[c, slot(2)].astype(F32)

        @pl.when(lane == 1)
        def _():
            to_y[c, slot(0)] = own[c, slot(2)].astype(BF16)
            r_ahead(c, 0).start()

    def red_3(c):
        r_across(c).wait_recv()

        @pl.when(lane == 0)
        def _():
            to_y[c, slot(0)] = (own[c, slot(2)] + from_x[c].astype(F32)).astype(BF16)
            r_ahead(c, 0).start()

        @pl.when(lane == 1)
        def _():
            own[c, slot(0)] += from_x[c].astype(F32)

        @pl.when(core == 1)
        def _():
            own[c, slot(0)] += from_sib[c, slot(0)].astype(F32)

    def red_4(c):
        r_ahead(c, 0).wait_recv()
        text_grad[slot(c)] = (own[c, slot(0)] + from_y[c, slot(0)].astype(F32)).astype(BF16)

    loss_sum[...] = jnp.zeros_like(loss_sum)
    stages = (dist_start, dist_second, dist_third, dist_late, compute, red_1, red_2, red_3, red_4)
    order = sorted((c + when, i, c) for i, when in enumerate(STAGES) for c in range(CHUNKS))
    for _, i, c in order:
        stages[i](c)
        if (i, c) == (0, 0):
            image_t[...] = image[...].T
        if (i, c) == (4, CHUNKS - 1):
            image_grad[...] = grad[...].astype(BF16)
            loss[...] = jnp.sum(loss_sum[...], axis=0, keepdims=True) * (1.0 / (STEPS * rows))

    for c in range(CHUNKS):
        d_back(c, 0).wait_send()
        d_back(c, 1).wait_send()
        d_across(c).wait_send()
        r_ahead(c, 0).wait_send()
        r_ahead(c, 1).wait_send()
        r_across(c).wait_send()

        @pl.when(core == 0)
        def _():
            d_back(c, 2).wait_send()
            r_ahead(c, 2).wait_send()

        for k in range(4):
            d_sib(c, k).wait_send()
            r_sib(c, k).wait_send()


def window_terms(scalars, offset, partner, image, text):
    rows, depth = image.shape
    size = rows // CHUNKS
    vmem = pl.BlockSpec(memory_space=pltpu.VMEM)
    smem = pl.BlockSpec(memory_space=pltpu.SMEM)
    return pl.pallas_call(
        kernel,
        name="window_terms",
        out_shape=(
            jax.ShapeDtypeStruct((1, rows), F32),
            jax.ShapeDtypeStruct((rows, depth), BF16),
            jax.ShapeDtypeStruct((rows, depth), BF16),
        ),
        in_specs=[smem, smem, vmem, vmem, vmem],
        out_specs=[vmem, vmem, vmem],
        scratch_shapes=[
            pltpu.VMEM((CHUNKS, 9 * size, depth), BF16),
            pltpu.VMEM((depth, rows), BF16),
            pltpu.VMEM((2 * size, rows), F32),
            pltpu.VMEM((8 * size, rows), BF16),
            pltpu.VMEM((rows, 8 * size), BF16),
            pltpu.VMEM((rows, depth), F32),
            pltpu.VMEM((CHUNKS, 4 * size, depth), F32),
            pltpu.VMEM((CHUNKS, 4 * size, depth), BF16),
            pltpu.VMEM((CHUNKS, 4 * size, depth), BF16),
            pltpu.VMEM((CHUNKS, 3 * size, depth), BF16),
            pltpu.VMEM((CHUNKS, size, depth), BF16),
            pltpu.VMEM((CHUNKS, 2 * size, depth), BF16),
            pltpu.VMEM((CHUNKS, size, depth), BF16),
            pltpu.VMEM((8, rows), F32),
            pltpu.SemaphoreType.DMA((CHUNKS, 8)),
            pltpu.SemaphoreType.DMA((CHUNKS, 8)),
            pltpu.SemaphoreType.DMA((CHUNKS, 8)),
            pltpu.SemaphoreType.DMA((CHUNKS, 8)),
        ],
        compiler_params=pltpu.CompilerParams(
            collective_id=0, has_side_effects=True, vmem_limit_bytes=60 * 2**20
        ),
        cost_estimate=pl.CostEstimate(
            flops=3 * 2 * STEPS * rows * rows * depth,
            bytes_accessed=8 * rows * depth,
            transcendentals=2 * STEPS * rows * rows,
        ),
    )(scalars, offset, partner, image, text)


def halves(x, n):
    return lax.div(x, n), lax.rem(x, n)


def home_of(block):
    chip, core = halves(block, 2)
    group, inside = halves(chip, 8)
    z, x_hi = halves(group, 2)
    step, lane = halves(inside, 2)
    y = lax.rem(step + x_hi * (3 - 2 * step) + 1, 4)
    x_lo = lane + x_hi * (1 - 2 * lane)
    return z * 32 + x_hi * 16 + core * 8 + y * 2 + x_lo


def block_at(row, col):
    z, rest = halves(row, 4)
    x_hi, core = halves(rest, 2)
    y, x_lo = halves(col, 2)
    y = lax.rem(y + 3, 4)
    step = y + x_hi * (3 - 2 * y)
    lane = x_lo + x_hi * (1 - 2 * x_lo)
    return z * 32 + x_hi * 16 + 4 * step + 2 * lane + core


def move_kernel(by, returns, source, target, local, send, recv):
    row, col = lax.axis_index("row"), lax.axis_index("col")
    here = row * 8 + col
    realigned = home_of(lax.rem(here + (BLOCKS - by), BLOCKS))
    original = lax.rem(block_at(row, col) + by, BLOCKS)
    to, fro = (original, realigned) if returns else (realigned, original)
    barrier = pltpu.get_barrier_semaphore()
    remote = pltpu.make_async_remote_copy(
        src_ref=source, dst_ref=target, send_sem=send, recv_sem=recv,
        device_id=halves(to, 8), device_id_type=MESH,
    )

    @pl.when(fro != here)
    def _():
        pl.semaphore_signal(barrier, inc=1, device_id=halves(fro, 8), device_id_type=MESH)

    @pl.when(to != here)
    def _():
        pl.semaphore_wait(barrier, 1)
        remote.start()
        remote.wait_send()

    @pl.when(to == here)
    def _():
        stays = pltpu.make_async_copy(source, target, local)
        stays.start()
        stays.wait()

    @pl.when(fro != here)
    def _():
        remote.wait_recv()


def moved_by(by, values, returns):
    anywhere = pl.BlockSpec(memory_space=pl.ANY)

    def branch(amount):
        return lambda v: pl.pallas_call(
            functools.partial(move_kernel, amount, returns),
            name="move",
            out_shape=jax.ShapeDtypeStruct(v.shape, v.dtype),
            in_specs=[anywhere],
            out_specs=anywhere,
            scratch_shapes=[pltpu.SemaphoreType.DMA] * 3,
            compiler_params=pltpu.CompilerParams(
                collective_id=1 + amount + returns * BLOCKS, has_side_effects=True
            ),
        )(v)

    return lax.switch(by, [branch(amount) for amount in range(BLOCKS)], values)


def on_device(image_embed, text_embed, partner, offset, log_scale, logit_bias):
    rows = image_embed.shape[0]
    start = offset % BLOCKS
    out = [(block, home(block)) for block in range(BLOCKS)]
    back = [(there, here) for here, there in out]
    image = lax.ppermute(image_embed, AXES, out)
    partner = lax.ppermute(partner, AXES, out)
    text = moved_by(start[0], text_embed, False)
    scalars = jnp.concatenate([jnp.exp(log_scale), logit_bias])
    loss, image_grad, text_grad = window_terms(scalars, start, partner.reshape(1, rows), image, text)
    row_loss = lax.ppermute(loss.reshape(rows), AXES, back)
    image_grad = lax.ppermute(image_grad, AXES, back)
    text_grad = moved_by(start[0], text_grad, True)
    return row_loss, image_grad, text_grad


def solution(mesh):
    return jax.shard_map(
        on_device,
        mesh=mesh,
        in_specs=(P(AXES, None), P(AXES, None), P(AXES), P(), P(), P()),
        out_specs=(P(AXES), P(AXES, None), P(AXES, None)),
        check_vma=False,
    )
```
